256 devices in a mesh: row: 16 (over x, y_hi, core), col: 16 (over y_lo, z).
Axes of the slice: x: 4, y: 4 (y_hi: 2, y_lo: 2; y = y_hi * 2 + y_lo), z: 8, core: 2. Of those that a mesh axis runs over, the one named last changes fastest.
Arguments:
- statistic: float32 [16384, 16384], P('row', 'col'), may hold values from -6 to 6
- gradient: bfloat16 [16384, 4096], P('row', 'col'), may hold values from -0.75 to 0.75
Outputs:
- updated: float32 [16384, 16384], P('row', 'col')
The draws below stay inside these ranges and needn't reach their ends.
All inputs are finite; a program needn't handle non-finite values.
Results may differ from the reference program's by a relative error of at most 0.0003.
Values may be sent and summed in bfloat16 or wider, within the bound.
A program may use at most 128 MiB of HBM per device.

```python
import jax
import jax.numpy as jnp
from jax import lax

MODEL_DIM = 16384
PANEL = 4096


def shard_levels(own_key, extent, cuts, low, high):
    def one(dim, shards_of):
        draws = jax.random.uniform(jax.random.fold_in(jax.random.fold_in(own_key, 6), dim), (shards_of,), jnp.float32, low / len(cuts), high / len(cuts))
        return jnp.repeat(jnp.exp(draws), extent[dim] // shards_of).reshape((-1,) + (1,) * (len(extent) - dim - 1))

    factor_of = one(*cuts[0])
    for cut in cuts[1:]:
        factor_of = factor_of * one(*cut)
    return factor_of


def gaussian(stream_key, dims, width, limit, split=(), kind=jnp.bfloat16):
    drawn = width * jax.random.normal(stream_key, dims, jnp.float32)
    if split:
        drawn = drawn * shard_levels(stream_key, dims, split, -0.22, 0.18)
    return jnp.clip(drawn, -limit, limit).astype(kind)


def setup_inputs(seed: int = 0) -> dict:
    splits = jax.random.split(jax.random.key(seed), 3)
    statistic = gaussian(splits[0], (MODEL_DIM, MODEL_DIM), 1.0, 6.0, ((0, 16), (1, 16)), jnp.float32)
    gradient = gaussian(splits[1], (MODEL_DIM, PANEL), 0.125, 0.75, ((0, 16), (1, 16)))
    return {"statistic": statistic, "gradient": gradient}


def reference(statistic, gradient):
    gradient_wide = gradient.astype(jnp.float32)
    product = jnp.dot(gradient_wide, gradient_wide.T, precision=lax.Precision.HIGHEST, preferred_element_type=jnp.float32)
    return statistic + product
```

```python
import functools

import jax
import jax.numpy as jnp
from jax import lax
from jax.experimental import pallas as pl
from jax.experimental.pallas import tpu as pltpu
from jax.sharding import PartitionSpec as P

MESH = pl.DeviceIdType.MESH
X, Y, Z = 4, 4, 8
TILES = 16
HALF = 512
DEPTH = 256
ROUNDS = 5
STEPS = 3 * ROUNDS
HOP = 2
LAG = 4 * HOP + 3


def device(x, y, z, core):
    return (x * 4 + (y // 2) * 2 + core, (y % 2) * Z + z)


def kernel(stat_ref, grad_ref, out_ref, rows, part, own_sem, stat_sem, rows_sem, part_sem, send_rows, send_twin, send_x, send_cross):
    r, c = lax.axis_index("row"), lax.axis_index("col")
    x, yh, core = r // 4, (r // 2) % 2, r % 2
    yl, z = c // Z, c % Z
    y = 2 * yh + yl
    first, second = core == 0, core == 1

    x_c, yh_c, core_c = c // 4, (c // 2) % 2, c % 2
    rel = (x - x_c + X) % X
    same = yh == yh_c
    root = same & (rel == 0)

    z_up, z_down = (x, y, (z + 1) % Z), (x, y, (z + Z - 1) % Z)
    mate = (x, 2 * yh + 1 - yl, z)
    twin = device(x, y, z, 1 - core)
    x_up, x_down = device((x + 1) % X, y, z, core), device((x + X - 1) % X, y, z, core)
    x_far = device((x + 2) % X, y, z, core)
    y_far = device(x, (y + 2) % Y, z, core)

    own = 2 * c
    load = [pltpu.make_async_copy(grad_ref.at[pl.ds(h * HALF, HALF)], rows.at[core, own + h], own_sem.at[h]) for h in range(2)]
    for copy in load:
        copy.start()
    stat = pltpu.make_async_copy(stat_ref, out_ref, stat_sem)
    stat.start()

    barrier = pltpu.get_barrier_semaphore()

    def greet(others):
        for other in others:
            pl.semaphore_signal(barrier, inc=1, device_id=other, device_id_type=MESH)
        pl.semaphore_wait(barrier, len(others))

    beside = [device(*at, 0) for at in (z_up, z_down, mate)]

    @pl.when(first)
    def _():
        greet([twin, *beside, *[device(*at, 1) for at in (z_up, z_down, mate)]])

    @pl.when(second)
    def _():
        greet([twin, *beside, x_up, x_down, x_far, y_far])

    for copy in load:
        copy.wait()

    def send_row(b, piece, to):
        pltpu.make_async_remote_copy(
            rows.at[b, piece], rows.at[b, piece], send_rows, rows_sem.at[b, piece], device_id=device(*to, 0), device_id_type=MESH
        ).start()

    def send_part(source, piece, to, sem):
        pltpu.make_async_remote_copy(source.at[piece], part.at[piece], sem, part_sem.at[piece], device_id=to, device_id_type=MESH).start()

    def wait_row(b, piece):
        pltpu.make_async_copy(rows.at[b, piece], rows.at[b, piece], rows_sem.at[b, piece]).wait()

    def wait_part(piece):
        pltpu.make_async_copy(part.at[piece], part.at[piece], part_sem.at[piece]).wait()

    def piece_of(far, mates, h):
        return 2 * (((yl + mates) % 2) * Z + (z + far + Z) % Z) + h

    def crosses_at(far, h):
        d = (far + Z) % Z
        return jnp.where(d < 2, 2, jnp.where((d == 3) | (d == 4), 0, 1 + 2 * h))

    def to_twin(b, piece):
        if b == 1:
            pltpu.make_async_remote_copy(
                rows.at[1, piece], rows.at[1, piece], send_twin, rows_sem.at[1, piece], device_id=twin, device_id_type=MESH
            ).start()

        @pl.when(root & (core_c == b))
        def _():
            send_part(rows.at[b], piece, twin, send_twin)

    def both(s, body):
        body(-s, True)

        @pl.when((s >= 1) & (s <= 3))
        def _():
            body(s, False)

    def gather(n):
        s, j = n // 3, n % 3
        h = jnp.where(j == 0, 1, 0)
        mates = jnp.where(j == 2, 1, 0)

        def one(b, far, up):
            piece = piece_of(far, mates, h)
            last_up = (j == 1) | ((j == 0) & (b == 0))

            def act():
                @pl.when((s >= 1) | (j == 2))
                def _():
                    wait_row(b, piece)

                if up:

                    @pl.when((s < 3) | ((s == 3) & last_up))
                    def _():
                        send_row(b, piece, z_up)

                    @pl.when(s == 0)
                    def _():
                        send_row(b, piece, z_down)
                else:

                    @pl.when((s < 3) | jnp.logical_not(last_up))
                    def _():
                        send_row(b, piece, z_down)

                @pl.when(j == 0)
                def _():
                    send_row(b, piece, mate)

                to_twin(b, piece)

            if b == 0:
                act()
            else:
                pl.when((s >= 1) | (j == 2))(act)

        def body(far, up):
            for b in range(2):
                one(b, far, up)

        both(s, body)

        @pl.when(j == 2)
        def _():
            def body(far, up):
                piece = piece_of(far, 1, 1)
                for b in range(2):
                    wait_row(b, piece)
                    to_twin(b, piece)

            both(s, body)

    lag = [jnp.where(same, HOP * (rel if h == 0 else (X - rel) % X), HOP * (1 + jnp.where(rel == 3, 1, rel))) for h in range(2)]

    def forward(far, mates, h):
        piece = piece_of(far, mates, h)
        here = crosses_at(far, h) == rel

        @pl.when(same | here)
        def _():
            wait_part(piece)

            @pl.when(same & (rel != (1 if h else 3)))
            def _():
                send_part(part, piece, x_down if h else x_up, send_x)

            @pl.when(same & here)
            def _():
                send_part(part, piece, y_far, send_cross)

            @pl.when(jnp.logical_not(same))
            def _():
                send_part(part, piece, x_up, send_x)
                send_part(part, piece, x_down, send_x)
                send_part(part, piece, x_far, send_x)

            send_part(part, piece, twin, send_twin)

    def accept(far, mates, h):
        piece = piece_of(far, mates, h)

        @pl.when(jnp.logical_not(same) & (crosses_at(far, h) != rel))
        def _():
            wait_part(piece)
            send_part(part, piece, twin, send_twin)

    def spread(n):
        for act, lags in ((forward, lag), (accept, [4 * HOP, 4 * HOP])):
            for h in range(2):
                m = n - lags[h]
                s, j = m // 3, m % 3

                @pl.when((m >= 0) & (m < STEPS) & (j == 1 - h))
                def _():
                    both(s, lambda far, up: act(far, 0, h))

                @pl.when((m >= 0) & (m < STEPS) & (j == 2))
                def _():
                    both(s, lambda far, up: act(far, 1, h))

    def multiply(far):
        for mates in range(2):
            for h in range(2):
                piece = piece_of(far, mates, h)
                pl.when(first)(functools.partial(wait_part, piece))
                pl.when(second & ((far != 0) | (mates != 0)))(functools.partial(wait_row, 1, piece))

        t0 = (z + far + Z) % Z
        t1 = Z + t0

        def block(i, carry):
            h, b = i // 4, i % 4
            cols = pl.ds(pl.multiple_of(b * DEPTH, DEPTH), DEPTH)
            at = pl.ds(pl.multiple_of(h * HALF, HALF), HALF)
            sub = pl.ds(pl.multiple_of((b % 2) * DEPTH, DEPTH), DEPTH)
            total = None
            for t in (t0, t1):
                term = lax.dot_general(
                    rows[core, 2 * t + h],
                    part[2 * t + b // 2, sub, :],
                    (((1,), (1,)), ((), ())),
                    preferred_element_type=jnp.float32,
                )
                total = term if total is None else total + term
            out_ref[at, cols] += total
            return carry

        lax.fori_loop(0, 8, block, 0)

    @pl.when(first)
    def _():
        send_row(0, own, mate)

    @pl.when(second)
    def _():
        send_row(1, own, mate)
        for h in (1, 0):
            for to in (z_up, z_down):
                send_row(1, own + h, to)
        send_row(1, own + 1, mate)

        @pl.when(root & (core_c == 1))
        def _():
            for h in range(2):
                pltpu.make_async_copy(rows.at[1, own + h], part.at[own + h], part_sem.at[own + h]).start()

    def step(n, carry):
        @pl.when(first & (n < STEPS))
        def _():
            gather(n)

        @pl.when(second)
        def _():
            spread(n)

        m = n - LAG

        @pl.when(m == 0)
        def _():
            stat.wait()

        s, j = m // 3, m % 3

        @pl.when((m >= 0) & (m < STEPS) & ((j == 0) | ((j == 1) & (s >= 1) & (s <= 3))))
        def _():
            multiply(jnp.where(j == 0, s, -s))

        return carry

    lax.fori_loop(0, STEPS + LAG, step, 0)

    def drain(sem, count):
        pltpu.make_async_copy(part.at[pl.ds(0, count)], part.at[pl.ds(0, count)], sem).wait()

    @pl.when(first)
    def _():
        pltpu.make_async_copy(rows.at[:, pl.ds(0, 27)], rows.at[:, pl.ds(0, 27)], send_rows).wait()

        @pl.when(root & (core_c == 0))
        def _():
            pltpu.make_async_copy(rows.at[:, pl.ds(0, 31)], rows.at[:, pl.ds(0, 31)], send_twin).wait()

        @pl.when(root & (core_c == 1))
        def _():
            pltpu.make_async_copy(rows.at[:, pl.ds(0, 30)], rows.at[:, pl.ds(0, 30)], send_twin).wait()

        @pl.when(jnp.logical_not(root))
        def _():
            drain(send_twin, 30)

    @pl.when(second)
    def _():
        drain(send_rows, 6)
        drain(send_twin, 32)

        @pl.when(same)
        def _():
            drain(send_cross, 8)

            @pl.when(rel % 2 == 0)
            def _():
                drain(send_x, 32)

            @pl.when(rel % 2 == 1)
            def _():
                drain(send_x, 16)

        @pl.when(jnp.logical_not(same))
        def _():
            drain(send_x, 24)


def local(statistic, gradient):
    return pl.pallas_call(
        kernel,
        out_shape=jax.ShapeDtypeStruct(statistic.shape, jnp.float32),
        in_specs=[pl.BlockSpec(memory_space=pl.ANY)] * 2,
        out_specs=pl.BlockSpec(memory_space=pltpu.VMEM),
        scratch_shapes=[
            pltpu.VMEM((2, 2 * TILES, HALF, DEPTH), jnp.bfloat16),
            pltpu.VMEM((2 * TILES, HALF, DEPTH), jnp.bfloat16),
            pltpu.SemaphoreType.DMA((2,)),
            pltpu.SemaphoreType.DMA,
            pltpu.SemaphoreType.DMA((2, 2 * TILES)),
            pltpu.SemaphoreType.DMA((2 * TILES,)),
            pltpu.SemaphoreType.DMA,
            pltpu.SemaphoreType.DMA,
            pltpu.SemaphoreType.DMA,
            pltpu.SemaphoreType.DMA,
        ],
        compiler_params=pltpu.CompilerParams(collective_id=0, has_side_effects=True, vmem_limit_bytes=60 << 20),
        cost_estimate=pl.CostEstimate(flops=2 * 1024 * 1024 * 4096, bytes_accessed=9 << 20, transcendentals=0),
        name="shampoo",
    )(statistic, gradient)


def solution(mesh):
    spec = P("row", "col")
    return jax.shard_map(local, mesh=mesh, in_specs=(spec, spec), out_specs=spec, check_vma=False)
```

```python
import functools

import jax
import jax.numpy as jnp
from jax import lax
from jax.experimental import pallas as pl
from jax.experimental.pallas import tpu as pltpu
from jax.sharding import PartitionSpec as P

MESH = pl.DeviceIdType.MESH
X, Y, Z = 4, 4, 8
TILES = 16
HALF = 512
DEPTH = 256
ROUNDS = 5
STEPS = 2 * ROUNDS
LAG = 2
HOP = 2
SPLIT = 2
PIECE = HALF // SPLIT
FIRST_AT, SECOND_AT = 11, 6
ORDER = (
    (1, -1, 2, -1, 3, 5, 6, 7, 0, 4),
    (1, 2, -1, 3, -1, 0, 5, 6, 7, 4),
)


def device(x, y, z, core):
    return (x * 4 + (y // 2) * 2 + core, (y % 2) * Z + z)


def kernel(stat_ref, grad_ref, out_ref, rows, part, own_sem, stat_sem, rows_sem, part_sem, send_rows, send_twin, send_x, send_cross):
    r, c = lax.axis_index("row"), lax.axis_index("col")
    x, yh, core = r // 4, (r // 2) % 2, r % 2
    yl, z = c // Z, c % Z
    y = 2 * yh + yl
    first, second = core == 0, core == 1

    x_c, yh_c, core_c = c // 4, (c // 2) % 2, c % 2
    rel = (x - x_c + X) % X
    same = yh == yh_c
    root = same & (rel == 0)

    z_up, z_down = (x, y, (z + 1) % Z), (x, y, (z + Z - 1) % Z)
    mate = (x, 2 * yh + 1 - yl, z)
    twin = device(x, y, z, 1 - core)
    x_up, x_down = device((x + 1) % X, y, z, core), device((x + X - 1) % X, y, z, core)

    x_m = (1 - yl) * 2 + z // 4
    relay = same & (x == x_m)
    z_of = [(x % 2) * 4 + yh * 2 + b for b in range(2)]
    across = [((x + d) % X, 2 * (1 - yh) + 1 - yl, z) for d in (0, 1, X - 1)]

    own = 2 * SPLIT * c
    load = [
        pltpu.make_async_copy(grad_ref.at[pl.ds(u * PIECE, PIECE)], rows.at[core, own + u], own_sem.at[u]) for u in range(2 * SPLIT)
    ]
    for copy in load:
        copy.start()
    stat = pltpu.make_async_copy(stat_ref, out_ref, stat_sem)
    stat.start()

    barrier = pltpu.get_barrier_semaphore()

    def greet(others):
        for other in others:
            pl.semaphore_signal(barrier, inc=1, device_id=other, device_id_type=MESH)
        pl.semaphore_wait(barrier, len(others))

    beside = [device(*at, 0) for at in (z_up, z_down, mate)]

    @pl.when(first)
    def _():
        greet([twin, *beside, *[device(*at, 1) for at in (z_up, z_down, mate, *across)]])

    @pl.when(second)
    def _():
        greet([twin, *beside, x_up, x_down, *[device(*at, k) for at in across for k in range(2)]])

    for copy in load:
        copy.wait()

    def send_row(b, piece, to):
        pltpu.make_async_remote_copy(
            rows.at[b, piece], rows.at[b, piece], send_rows, rows_sem.at[b, piece], device_id=device(*to, 0), device_id_type=MESH
        ).start()

    def send_part(source, piece, to, sem):
        pltpu.make_async_remote_copy(source.at[piece], part.at[piece], sem, part_sem.at[piece], device_id=to, device_id_type=MESH).start()

    def wait_row(b, piece):
        pltpu.make_async_copy(rows.at[b, piece], rows.at[b, piece], rows_sem.at[b, piece]).wait()

    def wait_part(piece):
        pltpu.make_async_copy(part.at[piece], part.at[piece], part_sem.at[piece]).wait()

    def piece_of(far, mates, h):
        return SPLIT * (2 * (((yl + mates) % 2) * Z + (z + far + Z) % Z) + h)

    def aside(far):
        d = (far + Z) % Z
        return (d >= 1) & (d <= 3)

    def pass_on(b, far, piece, h):
        if b == 1:
            pltpu.make_async_remote_copy(
                rows.at[1, piece], rows.at[1, piece], send_twin, rows_sem.at[1, piece], device_id=twin, device_id_type=MESH
            ).start()

        @pl.when(root & (core_c == b))
        def _():
            send_part(rows.at[b], piece, twin, send_twin)

        @pl.when(relay & (core_c == b))
        def _():
            beside_it = aside(far)

            @pl.when(jnp.logical_not(beside_it))
            def _():
                send_part(rows.at[b], piece, device(*across[0], 1), send_cross)

            @pl.when(beside_it & (h == 0))
            def _():
                send_part(rows.at[b], piece, device(*across[1], 1), send_cross)

            @pl.when(beside_it & (h == 1))
            def _():
                send_part(rows.at[b], piece, device(*across[2], 1), send_cross)

    def both(s, body):
        body(-s, True)

        @pl.when((s >= 1) & (s <= 3))
        def _():
            body(s, False)

    def ring(b, s, up, piece, last_up, skip):
        if up:

            @pl.when(((s < 3) | ((s == 3) & last_up)) & jnp.logical_not(skip & ((z + 1) % Z == z_of[b])))
            def _():
                send_row(b, piece, z_up)

            @pl.when((s == 0) & jnp.logical_not(skip & ((z + Z - 1) % Z == z_of[b])))
            def _():
                send_row(b, piece, z_down)
        else:

            @pl.when(((s < 3) | jnp.logical_not(last_up)) & jnp.logical_not(skip & ((z + Z - 1) % Z == z_of[b])))
            def _():
                send_row(b, piece, z_down)

    def exchanged(b, s, j):
        return (s == 0) | jnp.where(j == 0, z != z_of[1 - b], z == z_of[b])

    def gather(n):
        s, j = n // 2, n % 2
        h = 1 - j

        def body(far, up):
            for b in range(2):

                def act(b=b):
                    for u in range(SPLIT):
                        piece = piece_of(far, 0, h) + u

                        @pl.when(s >= 1)
                        def _():
                            wait_row(b, piece)

                        ring(b, s, up, piece, (j == 0) if b == 0 else (j == 1), False)

                        @pl.when(exchanged(b, s, j))
                        def _():
                            send_row(b, piece, mate)

                        pass_on(b, far, piece, h)

                if b == 0:
                    act()
                else:
                    pl.when(s >= 1)(act)

        @pl.when(n < STEPS)
        def _():
            both(s, body)

        def crossed(far, up):
            for b in range(2):

                @pl.when(exchanged(b, s - LAG // 2, j))
                def _():
                    for u in range(SPLIT):
                        piece = piece_of(far, 1, h) + u
                        wait_row(b, piece)
                        pass_on(b, far, piece, h)

        @pl.when(n >= LAG)
        def _():
            both(s - LAG // 2, crossed)

    def deferred(act):
        for b in range(2):

            @pl.when(z == z_of[1 - b])
            def _():
                def one(far, carry):
                    for u in range(SPLIT):
                        act(b, far, u)
                    return carry

                lax.fori_loop(1, Z, one, 0)

    def gather_rest(s):
        def body(far, up):
            for b in range(2):
                for u in range(SPLIT):
                    piece = piece_of(far, 1, 0) + u

                    @pl.when((s >= 1) & (z != z_of[b]))
                    def _():
                        wait_row(b, piece)

                    ring(b, s, up, piece, b == 0, True)

                    if b == 1:

                        @pl.when((s >= 1) & (z != z_of[b]))
                        def _():
                            pass_on(b, far, piece, 0)

        both(s, body)

    lag = [HOP * (jnp.where(same, 0, 1) + (rel if h == 0 else (X - rel) % X)) for h in range(2)]
    other = jnp.logical_not(same)
    early = jnp.where(same, 0, 1)

    def forward(far, mates, h):
        beside_it = other & aside(far)
        entry = jnp.where(beside_it, 1, 0)
        hop = (rel - entry + X) % X if h == 0 else (2 * X - entry - rel) % X

        @pl.when(jnp.logical_not(beside_it & (rel == 0)))
        def _():
            for u in range(SPLIT):
                piece = piece_of(far, mates, h) + u
                wait_part(piece)

                @pl.when(hop < X - 1 - entry)
                def _():
                    send_part(part, piece, x_down if h else x_up, send_x)

                @pl.when(beside_it & (hop == 0))
                def _():
                    send_part(part, piece, x_up if h else x_down, send_x)

                send_part(part, piece, twin, send_twin)

    def accept(far, mates, h):
        @pl.when(other & aside(far) & (rel == 0))
        def _():
            for u in range(SPLIT):
                piece = piece_of(far, mates, h) + u
                wait_part(piece)
                send_part(part, piece, twin, send_twin)

    def spread(n):
        for act, lags in ((forward, lag), (accept, [3 * HOP, 3 * HOP])):
            for h in range(2):
                m = n - lags[h]

                @pl.when((m >= 0) & (m < STEPS) & (m % 2 == 1 - h))
                def _():
                    both(m // 2, lambda far, up: act(far, early, h))

                @pl.when((m >= LAG) & (m < STEPS + LAG) & (m % 2 == 1 - h))
                def _():
                    both((m - LAG) // 2, lambda far, up: act(far, 1 - early, h))

    def multiply(mates, far):
        ends = (far, jnp.where(far == 0, 4, -far))
        for end in ends:
            tile = piece_of(end, mates, 0)

            @pl.when(first)
            def _():
                for u in range(2 * SPLIT):
                    wait_part(tile + u)

            @pl.when(second & ((end != 0) | (mates != 0)))
            def _():
                for u in range(2 * SPLIT):
                    wait_row(1, tile + u)

        def tiles(ref, *lead):
            return jnp.concatenate(
                [ref[*lead, pl.ds(piece_of(end, mates, 0), 2 * SPLIT)].reshape(2 * HALF, DEPTH) for end in ends], axis=1
            )

        out_ref[...] += lax.dot_general(
            tiles(rows, core), tiles(part), (((1,), (1,)), ((), ())), preferred_element_type=jnp.float32
        )

    @pl.when(second)
    def _():
        for u in (*range(SPLIT, 2 * SPLIT), *range(SPLIT)):
            for to in (z_up, z_down, mate):
                send_row(1, own + u, to)

        @pl.when(root & (core_c == 1))
        def _():
            for u in range(2 * SPLIT):
                pltpu.make_async_copy(rows.at[1, own + u], part.at[own + u], part_sem.at[own + u]).start()

        @pl.when(relay & (core_c == 1))
        def _():
            for u in range(2 * SPLIT):
                send_part(rows.at[1], own + u, device(*across[0], 1), send_cross)

    lag_most = jnp.where(other & (rel == 0), 3 * HOP, jnp.maximum(lag[0], lag[1]))
    rest = STEPS + LAG

    def step(n, carry):
        @pl.when(first & (n < rest))
        def _():
            gather(n)

        @pl.when(first & (n == rest))
        def _():
            deferred(lambda b, far, u: send_row(b, piece_of(far, 0, 1) + u, mate))

        @pl.when(first & (n >= rest) & (n < rest + ROUNDS))
        def _():
            gather_rest(n - rest)

        @pl.when(first & (n == rest + ROUNDS - 1))
        def _():
            def late(b, far, u):
                piece = piece_of(far, 1, 1) + u
                wait_row(b, piece)
                if b == 1:
                    pass_on(b, far, piece, 1)

            deferred(late)

        @pl.when(second)
        def _():
            spread(n)

        m = jnp.where(first, n - FIRST_AT, n - lag_most - SECOND_AT)

        @pl.when(m == 0)
        def _():
            stat.wait()

        turn = jnp.where(first, ORDER[0][-1], ORDER[1][-1])
        for i in range(len(ORDER[0])):
            turn = jnp.where(m == i, jnp.where(first, ORDER[0][i], ORDER[1][i]), turn)

        @pl.when((m >= 0) & (m < len(ORDER[0])) & (turn >= 0))
        def _():
            multiply(turn // 4, turn % 4)

        return carry

    lax.fori_loop(0, STEPS + LAG + 4 * HOP + 8, step, 0)

    def drain(sem, count):
        pltpu.make_async_copy(part.at[pl.ds(0, count * SPLIT)], part.at[pl.ds(0, count * SPLIT)], sem).wait()

    @pl.when(first)
    def _():
        place = (z - z_of[0] + Z) % Z
        more, fewer = place <= 1, (place == 2) | (place == Z - 1)
        for those, count in ((more, 29), (fewer, 25), (jnp.logical_not(more | fewer), 27)):

            @pl.when(those)
            def _():
                half = rows.at[:, pl.ds(0, count * SPLIT)]
                pltpu.make_async_copy(half, half, send_rows).wait()

        @pl.when(root & (core_c == 0))
        def _():
            pltpu.make_async_copy(rows.at[:, pl.ds(0, 31 * SPLIT)], rows.at[:, pl.ds(0, 31 * SPLIT)], send_twin).wait()

        @pl.when(root & (core_c == 1))
        def _():
            pltpu.make_async_copy(rows.at[:, pl.ds(0, 30 * SPLIT)], rows.at[:, pl.ds(0, 30 * SPLIT)], send_twin).wait()

        @pl.when(jnp.logical_not(root))
        def _():
            drain(send_twin, 30)

        @pl.when(relay & (core_c == 0))
        def _():
            drain(send_cross, 32)

        @pl.when(relay & (core_c == 1))
        def _():
            drain(send_cross, 30)

    @pl.when(second)
    def _():
        drain(send_rows, 6)
        drain(send_twin, 32)

        @pl.when(relay & (core_c == 1))
        def _():
            drain(send_cross, 2)

        for at, count, beyond in ((0, 32, 20), (1, 16, 22), (2, 32, 32), (3, 16, 22)):

            @pl.when(same & (rel == at))
            def _():
                drain(send_x, count)

            @pl.when(other & (rel == at))
            def _():
                drain(send_x, beyond)


def local(statistic, gradient):
    return pl.pallas_call(
        kernel,
        out_shape=jax.ShapeDtypeStruct(statistic.shape, jnp.float32),
        in_specs=[pl.BlockSpec(memory_space=pltpu.HBM)] * 2,
        out_specs=pl.BlockSpec(memory_space=pltpu.VMEM),
        scratch_shapes=[
            pltpu.VMEM((2, 2 * SPLIT * TILES, PIECE, DEPTH), jnp.bfloat16),
            pltpu.VMEM((2 * SPLIT * TILES, PIECE, DEPTH), jnp.bfloat16),
            pltpu.SemaphoreType.DMA((2 * SPLIT,)),
            pltpu.SemaphoreType.DMA,
            pltpu.SemaphoreType.DMA((2, 2 * SPLIT * TILES)),
            pltpu.SemaphoreType.DMA((2 * SPLIT * TILES,)),
            pltpu.SemaphoreType.DMA,
            pltpu.SemaphoreType.DMA,
            pltpu.SemaphoreType.DMA,
            pltpu.SemaphoreType.DMA,
        ],
        compiler_params=pltpu.CompilerParams(collective_id=0, has_side_effects=True, vmem_limit_bytes=48 << 20),
        cost_estimate=pl.CostEstimate(flops=2 * 1024 * 1024 * 4096, bytes_accessed=9 << 20, transcendentals=0),
        name="shampoo",
    )(statistic, gradient)


def solution(mesh):
    spec = P("row", "col")
    return jax.shard_map(local, mesh=mesh, in_specs=(spec, spec), out_specs=spec, check_vma=False)
```

```python
import functools

import jax
import jax.numpy as jnp
from jax import lax
from jax.experimental import pallas as pl
from jax.experimental.pallas import tpu as pltpu
from jax.sharding import PartitionSpec as P

MESH = pl.DeviceIdType.MESH
X, Y, Z = 4, 4, 8
TILES = 16
HALF = 512
DEPTH = 256
ROUNDS = 5
STEPS = 2 * ROUNDS
LAG = 2
ASIDE = (1, 2, 3)
TWO_WAYS = (4, 5)
HOP = 2
SPLIT = 2
PIECE = HALF // SPLIT
FIRST_AT, SECOND_AT = 11, 5
ORDER = (
    (1, 2, 5, 6, 3, 7, 0, 4, -1, -1, -1, -1, -1, -1, -1),
    (1, 5, 2, 6, 3, 7, 0, 4, -1, -1, -1, -1, -1, -1, -1),
    (1, -1, 2, -1, 3, -1, 0, 5, 6, 7, 4, -1, -1, -1, -1),
    (-1, -1, -1, -1, -1, -1, -1, 1, 2, 3, 0, 5, 6, 7, 4),
)


def div(a, b):
    return lax.div(a, jnp.int32(b))


def mod(a, b):
    return lax.rem(a, jnp.int32(b))


def device(x, y, z, core):
    return (x * 4 + (y // 2) * 2 + core, (y % 2) * Z + z)


def kernel(stat_ref, grad_ref, out_ref, rows, part, own_sem, stat_sem, rows_sem, part_sem, send_rows, send_twin, send_x, send_cross):
    r, c = lax.axis_index("row"), lax.axis_index("col")
    x, yh, core = r // 4, (r // 2) % 2, r % 2
    yl, z = c // Z, c % Z
    y = 2 * yh + yl
    first, second = core == 0, core == 1

    x_c, yh_c, core_c = c // 4, (c // 2) % 2, c % 2
    rel = (x - x_c + X) % X
    same = yh == yh_c
    root = same & (rel == 0)

    z_up, z_down = (x, y, (z + 1) % Z), (x, y, (z + Z - 1) % Z)
    mate = (x, 2 * yh + 1 - yl, z)
    twin = device(x, y, z, 1 - core)
    x_up, x_down = device((x + 1) % X, y, z, core), device((x + X - 1) % X, y, z, core)

    x_m = (1 - yl) * 2 + z // 4
    relay = same & (x == x_m)
    z_of = [(x % 2) * 4 + yh * 2 + b for b in range(2)]
    across = [((x + d) % X, 2 * (1 - yh) + 1 - yl, z) for d in (0, 1, X - 1)]

    own = 2 * SPLIT * c
    load = [
        pltpu.make_async_copy(grad_ref.at[pl.ds(u * PIECE, PIECE)], rows.at[core, own + u], own_sem.at[u]) for u in range(2 * SPLIT)
    ]
    for copy in load:
        copy.start()
    stat = pltpu.make_async_copy(stat_ref, out_ref, stat_sem)
    stat.start()

    barrier = pltpu.get_barrier_semaphore()

    def greet(others):
        for other in others:
            pl.semaphore_signal(barrier, inc=1, device_id=other, device_id_type=MESH)
        pl.semaphore_wait(barrier, len(others))

    beside = [device(*at, 0) for at in (z_up, z_down, mate)]

    @pl.when(first)
    def _():
        greet([twin, *beside, *[device(*at, 1) for at in (z_up, z_down, mate, *across)]])

    @pl.when(second)
    def _():
        greet([twin, *beside, x_up, x_down, *[device(*at, k) for at in across for k in range(2)]])

    for copy in load:
        copy.wait()

    def send_row(b, piece, to):
        pltpu.make_async_remote_copy(
            rows.at[b, piece], rows.at[b, piece], send_rows, rows_sem.at[b, piece], device_id=device(*to, 0), device_id_type=MESH
        ).start()

    def send_part(source, piece, to, sem):
        pltpu.make_async_remote_copy(source.at[piece], part.at[piece], sem, part_sem.at[piece], device_id=to, device_id_type=MESH).start()

    def wait_row(b, piece):
        pltpu.make_async_copy(rows.at[b, piece], rows.at[b, piece], rows_sem.at[b, piece]).wait()

    def wait_part(piece):
        pltpu.make_async_copy(part.at[piece], part.at[piece], part_sem.at[piece]).wait()

    def piece_of(far, mates, h):
        return SPLIT * (2 * (mod(yl + mates, 2) * Z + mod(z + far + Z, Z)) + h)

    def aside(far):
        return functools.reduce(jnp.logical_or, [(far == d) | (far == d - Z) for d in ASIDE])

    def pass_on(b, far, piece, h):
        if b == 1:
            pltpu.make_async_remote_copy(
                rows.at[1, piece], rows.at[1, piece], send_twin, rows_sem.at[1, piece], device_id=twin, device_id_type=MESH
            ).start()

        @pl.when(root & (core_c == b))
        def _():
            send_part(rows.at[b], piece, twin, send_twin)

        @pl.when(relay & (core_c == b))
        def _():
            beside_it = aside(far)

            @pl.when(jnp.logical_not(beside_it))
            def _():
                send_part(rows.at[b], piece, device(*across[0], 1), send_cross)

            @pl.when(beside_it & (h == 0))
            def _():
                send_part(rows.at[b], piece, device(*across[1], 1), send_cross)

            @pl.when(beside_it & (h == 1))
            def _():
                send_part(rows.at[b], piece, device(*across[2], 1), send_cross)

    def both(s, body):
        body(-s, True)

        @pl.when((s >= 1) & (s <= 3))
        def _():
            body(s, False)

    def ring(b, s, up, piece, last_up, skip):
        if up:

            @pl.when(((s < 3) | ((s == 3) & last_up)) & jnp.logical_not(skip & ((z + 1) % Z == z_of[b])))
            def _():
                send_row(b, piece, z_up)

            @pl.when((s == 0) & jnp.logical_not(skip & ((z + Z - 1) % Z == z_of[b])))
            def _():
                send_row(b, piece, z_down)
        else:

            @pl.when(((s < 3) | jnp.logical_not(last_up)) & jnp.logical_not(skip & ((z + Z - 1) % Z == z_of[b])))
            def _():
                send_row(b, piece, z_down)

    def exchanged(b, s, j):
        return (s == 0) | jnp.where(j == 0, z != z_of[1 - b], z == z_of[b])

    def gather(n):
        s, j = div(n, 2), mod(n, 2)
        h = 1 - j

        def body(far, up):
            for b in range(2):

                def act(b=b):
                    for u in range(SPLIT):
                        piece = piece_of(far, 0, h) + u

                        @pl.when(s >= 1)
                        def _():
                            wait_row(b, piece)

                        ring(b, s, up, piece, (j == 0) if b == 0 else (j == 1), False)

                        @pl.when(exchanged(b, s, j))
                        def _():
                            send_row(b, piece, mate)

                        pass_on(b, far, piece, h)

                if b == 0:
                    act()
                else:
                    pl.when(s >= 1)(act)

        @pl.when(n < STEPS)
        def _():
            both(s, body)

        def crossed(far, up):
            for b in range(2):

                @pl.when(z == z_of[b])
                def _():
                    for u in range(SPLIT):
                        piece = piece_of(far, 1, h) + u
                        wait_row(b, piece)
                        pass_on(b, far, piece, h)

        @pl.when((n >= LAG) & (n < STEPS + LAG))
        def _():
            both(s - LAG // 2, crossed)

    def deferred(act, spans):
        for b, (start, stop) in enumerate(spans):

            @pl.when(z == z_of[1 - b])
            def _():
                def one(far, carry):
                    @pl.when(far != Z)
                    def _():
                        for u in range(SPLIT):
                            act(b, far, u)

                    return carry

                lax.fori_loop(start, stop, one, 0)

    def gather_rest(s):
        def body(far, up):
            for b in range(2):
                for u in range(SPLIT):
                    piece = piece_of(far, 1, 0) + u

                    @pl.when(z != z_of[b])
                    def _():
                        wait_row(b, piece)

                    ring(b, s, up, piece, b == 0, True)

                    if b == 1:

                        @pl.when(z != z_of[b])
                        def _():
                            pass_on(b, far, piece, 0)

                @pl.when((z != z_of[b]) & ((s == 0) | (z != z_of[1 - b])))
                def _():
                    for u in range(SPLIT):
                        piece = piece_of(far, 1, 1) + u
                        wait_row(b, piece)

                        @pl.when((z_to[b] == z_of[1 - b]) & (s <= 2) & (far != 2 * b - 1))
                        def _():
                            send_row(b, piece, z_up if b == 1 else z_down)

                        if b == 1:
                            pass_on(b, far, piece, 1)

        z_to = ((z + Z - 1) % Z, (z + 1) % Z)
        both(s, body)

    lag = [HOP * (jnp.where(same, 0, 1) + (rel if h == 0 else (X - rel) % X)) for h in range(2)]
    other = jnp.logical_not(same)
    early = jnp.where(same, 0, 1)

    def forward(far, mates, h):
        beside_it = other & aside(far)
        entry = jnp.where(beside_it, 1, 0)
        two_ways = beside_it
        for d in TWO_WAYS:
            two_ways |= (far == d) | (far == d - Z)
        hop = mod(rel - entry + X, X) if h == 0 else mod(2 * X - entry - rel, X)

        @pl.when(jnp.logical_not(beside_it & (rel == 0)))
        def _():
            for u in range(SPLIT):
                piece = piece_of(far, mates, h) + u
                wait_part(piece)

                @pl.when(hop < jnp.where(two_ways, X - 2, X - 1))
                def _():
                    send_part(part, piece, x_down if h else x_up, send_x)

                @pl.when(two_ways & (hop == 0))
                def _():
                    send_part(part, piece, x_up if h else x_down, send_x)

                send_part(part, piece, twin, send_twin)

    def accept(far, mates, h):
        @pl.when(other & aside(far) & (rel == 0))
        def _():
            for u in range(SPLIT):
                piece = piece_of(far, mates, h) + u
                wait_part(piece)
                send_part(part, piece, twin, send_twin)

    def spread(n):
        for act, lags in ((forward, lag), (accept, [3 * HOP, 3 * HOP])):
            for h in range(2):
                m = n - lags[h]
                parity = mod(m + 64, 2)

                @pl.when((m >= 0) & (m < STEPS) & (parity == 1 - h))
                def _():
                    both(div(m, 2), lambda far, up: act(far, early, h))

                @pl.when((m >= LAG) & (m < STEPS + LAG) & (parity == 1 - h))
                def _():
                    both(div(m - LAG, 2), lambda far, up: act(far, 1 - early, h))

    def multiply(mates, far):
        ends = (far, jnp.where(far == 0, 4, -far))
        for end in ends:
            tile = piece_of(end, mates, 0)

            @pl.when(first)
            def _():
                for u in range(2 * SPLIT):
                    wait_part(tile + u)

            @pl.when(second & ((end != 0) | (mates != 0)))
            def _():
                for u in range(2 * SPLIT):
                    wait_row(1, tile + u)

        def tiles(ref, *lead):
            return jnp.concatenate(
                [ref[*lead, pl.ds(piece_of(end, mates, 0), 2 * SPLIT)].reshape(2 * HALF, DEPTH) for end in ends], axis=1
            )

        out_ref[...] += lax.dot_general(
            tiles(rows, core), tiles(part), (((1,), (1,)), ((), ())), preferred_element_type=jnp.float32
        )

    @pl.when(second)
    def _():
        for u in (*range(SPLIT, 2 * SPLIT), *range(SPLIT)):
            for to in (z_up, z_down, mate):
                send_row(1, own + u, to)

        @pl.when(root & (core_c == 1))
        def _():
            for u in range(2 * SPLIT):
                pltpu.make_async_copy(rows.at[1, own + u], part.at[own + u], part_sem.at[own + u]).start()

        @pl.when(relay & (core_c == 1))
        def _():
            for u in range(2 * SPLIT):
                send_part(rows.at[1], own + u, device(*across[0], 1), send_cross)

    lag_most = jnp.where(other & (rel == 0), 3 * HOP, jnp.maximum(lag[0], lag[1]))
    rest = STEPS - 2

    def step(n, carry):
        @pl.when(first & (n < STEPS + LAG))
        def _():
            gather(n)

        @pl.when(first & (n >= rest) & (n < rest + ROUNDS))
        def _():
            gather_rest(n - rest)

        @pl.when(first & (n == STEPS))
        def _():
            deferred(lambda b, far, u: send_row(b, piece_of(far, 0, 1) + u, mate), ((4, 7), (2, 5)))

        def late(b, far, u):
            piece = piece_of(far, 1, 1) + u
            wait_row(b, piece)
            if b == 1:
                pass_on(b, far, piece, 1)

        @pl.when(first & (n == STEPS + LAG - 1))
        def _():
            deferred(late, ((7, 12), (5, 10)))

        @pl.when(first & (n == STEPS + LAG))
        def _():
            deferred(late, ((4, 7), (2, 5)))

        @pl.when(second)
        def _():
            spread(n)

        m = jnp.where(first, n - FIRST_AT, n - lag_most - SECOND_AT)

        @pl.when(m == 0)
        def _():
            stat.wait()

        turn = jnp.full((), -1, jnp.int32)
        for i, turns in enumerate(zip(*ORDER)):
            now = jnp.where(first, turns[0], jnp.where(root, turns[3], jnp.where(z == z_of[0], turns[2], turns[1])))
            turn = jnp.where(m == i, now, turn)

        @pl.when(turn >= 0)
        def _():
            multiply(div(turn, 4), mod(turn, 4))

        return carry

    lax.fori_loop(0, STEPS + LAG + 4 * HOP + 8, step, 0)

    def drain(sem, count):
        half = rows.at[:, pl.ds(0, count // 2 * SPLIT)]
        pltpu.make_async_copy(half, half, sem).wait()

    @pl.when(first)
    def _():
        half = rows.at[:, pl.ds(0, 27 * SPLIT)]
        pltpu.make_async_copy(half, half, send_rows).wait()

        @pl.when(root & (core_c == 0))
        def _():
            pltpu.make_async_copy(rows.at[:, pl.ds(0, 31 * SPLIT)], rows.at[:, pl.ds(0, 31 * SPLIT)], send_twin).wait()

        @pl.when(root & (core_c == 1))
        def _():
            pltpu.make_async_copy(rows.at[:, pl.ds(0, 30 * SPLIT)], rows.at[:, pl.ds(0, 30 * SPLIT)], send_twin).wait()

        @pl.when(jnp.logical_not(root))
        def _():
            drain(send_twin, 30)

        @pl.when(relay & (core_c == 0))
        def _():
            drain(send_cross, 32)

        @pl.when(relay & (core_c == 1))
        def _():
            drain(send_cross, 30)

    @pl.when(second)
    def _():
        drain(send_rows, 6)
        drain(send_twin, 32)

        @pl.when(relay & (core_c == 1))
        def _():
            drain(send_cross, 2)

        both_ways, aside_all = 4 * len(TWO_WAYS), 4 * len(ASIDE)
        for at, count, beyond in ((0, 32 + both_ways, 32 + both_ways - aside_all), (1, 16, 16 + aside_all // 2), (2, 32 - both_ways, 32 - both_ways), (3, 16, 16 + aside_all // 2)):

            @pl.when(same & (rel == at))
            def _():
                drain(send_x, count)

            @pl.when(other & (rel == at))
            def _():
                drain(send_x, beyond)


def local(statistic, gradient):
    return pl.pallas_call(
        kernel,
        out_shape=jax.ShapeDtypeStruct(statistic.shape, jnp.float32),
        in_specs=[pl.BlockSpec(memory_space=pltpu.HBM)] * 2,
        out_specs=pl.BlockSpec(memory_space=pltpu.VMEM),
        scratch_shapes=[
            pltpu.VMEM((2, 2 * SPLIT * TILES, PIECE, DEPTH), jnp.bfloat16),
            pltpu.VMEM((2 * SPLIT * TILES, PIECE, DEPTH), jnp.bfloat16),
            pltpu.SemaphoreType.DMA((2 * SPLIT,)),
            pltpu.SemaphoreType.DMA,
            pltpu.SemaphoreType.DMA((2, 2 * SPLIT * TILES)),
            pltpu.SemaphoreType.DMA((2 * SPLIT * TILES,)),
            pltpu.SemaphoreType.DMA,
            pltpu.SemaphoreType.DMA,
            pltpu.SemaphoreType.DMA,
            pltpu.SemaphoreType.DMA,
        ],
        compiler_params=pltpu.CompilerParams(collective_id=0, has_side_effects=True, vmem_limit_bytes=48 << 20),
        cost_estimate=pl.CostEstimate(flops=2 * 1024 * 1024 * 4096, bytes_accessed=9 << 20, transcendentals=0),
        name="shampoo",
    )(statistic, gradient)


def solution(mesh):
    spec = P("row", "col")
    return jax.shard_map(local, mesh=mesh, in_specs=(spec, spec), out_specs=spec, check_vma=False)
```

```python
import functools

import jax
import jax.numpy as jnp
from jax import lax
from jax.experimental import pallas as pl
from jax.experimental.pallas import tpu as pltpu
from jax.sharding import PartitionSpec as P

MESH = pl.DeviceIdType.MESH
X, Y, Z = 4, 4, 8
TILES = 16
HALF = 512
DEPTH = 256
ROUNDS = 5
STEPS = 2 * ROUNDS
LAG = 2
ASIDE = ((1, 2, 3), (1, 2, 3))
TWO_WAYS = ((4, 5), (4,))
HOP = 2
SPLIT = 2
PIECE = HALF // SPLIT
FIRST_AT, SECOND_AT = 11, 5
ORDER = (
    (1, 2, 5, 6, 3, 7, 0, 4, -1, -1, -1, -1, -1, -1, -1),
    (1, 5, 2, 6, 3, 7, 0, 4, -1, -1, -1, -1, -1, -1, -1),
    (1, -1, 2, -1, 3, -1, 0, 5, 6, 7, 4, -1, -1, -1, -1),
    (-1, -1, -1, -1, -1, -1, -1, 1, 2, 3, 0, 5, 6, 7, 4),
)


def div(a, b):
    return lax.div(a, jnp.int32(b))


def mod(a, b):
    return lax.rem(a, jnp.int32(b))


def device(x, y, z, core):
    return (x * 4 + (y // 2) * 2 + core, (y % 2) * Z + z)


def kernel(stat_ref, grad_ref, out_ref, rows, part, own_sem, stat_sem, rows_sem, part_sem, send_rows, send_twin, send_x, send_cross):
    r, c = lax.axis_index("row"), lax.axis_index("col")
    x, yh, core = r // 4, (r // 2) % 2, r % 2
    yl, z = c // Z, c % Z
    y = 2 * yh + yl
    first, second = core == 0, core == 1

    x_c, yh_c, core_c = c // 4, (c // 2) % 2, c % 2
    rel = (x - x_c + X) % X
    same = yh == yh_c
    root = same & (rel == 0)

    z_up, z_down = (x, y, (z + 1) % Z), (x, y, (z + Z - 1) % Z)
    mate = (x, 2 * yh + 1 - yl, z)
    twin = device(x, y, z, 1 - core)
    x_up, x_down = device((x + 1) % X, y, z, core), device((x + X - 1) % X, y, z, core)

    x_m = (1 - yl) * 2 + z // 4
    relay = same & (x == x_m)
    z_of = [(x % 2) * 4 + yh * 2 + b for b in range(2)]
    across = [((x + d) % X, 2 * (1 - yh) + 1 - yl, z) for d in (0, 1, X - 1)]

    own = 2 * SPLIT * c
    load = [
        pltpu.make_async_copy(grad_ref.at[pl.ds(u * PIECE, PIECE)], rows.at[core, own + u], own_sem.at[u]) for u in range(2 * SPLIT)
    ]
    for copy in load:
        copy.start()
    stat = pltpu.make_async_copy(stat_ref, out_ref, stat_sem)
    stat.start()

    barrier = pltpu.get_barrier_semaphore()

    def greet(others):
        for other in others:
            pl.semaphore_signal(barrier, inc=1, device_id=other, device_id_type=MESH)
        pl.semaphore_wait(barrier, len(others))

    beside = [device(*at, 0) for at in (z_up, z_down, mate)]

    @pl.when(first)
    def _():
        greet([twin, *beside, *[device(*at, 1) for at in (z_up, z_down, mate, *across)]])

    @pl.when(second)
    def _():
        greet([twin, *beside, x_up, x_down, *[device(*at, k) for at in across for k in range(2)]])

    for copy in load:
        copy.wait()

    def send_row(b, piece, to):
        pltpu.make_async_remote_copy(
            rows.at[b, piece], rows.at[b, piece], send_rows, rows_sem.at[b, piece], device_id=device(*to, 0), device_id_type=MESH
        ).start()

    def send_part(source, piece, to, sem):
        pltpu.make_async_remote_copy(source.at[piece], part.at[piece], sem, part_sem.at[piece], device_id=to, device_id_type=MESH).start()

    def wait_row(b, piece):
        pltpu.make_async_copy(rows.at[b, piece], rows.at[b, piece], rows_sem.at[b, piece]).wait()

    def wait_part(piece):
        pltpu.make_async_copy(part.at[piece], part.at[piece], part_sem.at[piece]).wait()

    def piece_of(far, mates, h):
        return SPLIT * (2 * (mod(yl + mates, 2) * Z + mod(z + far + Z, Z)) + h)

    def among(far, distances):
        return functools.reduce(jnp.logical_or, [(far == d) | (far == d - Z) for d in distances], False)

    def aside(far, h):
        if isinstance(h, int):
            return among(far, ASIDE[h])
        return jnp.where(h == 0, among(far, ASIDE[0]), among(far, ASIDE[1]))

    def pass_on(b, far, piece, h):
        if b == 1:
            pltpu.make_async_remote_copy(
                rows.at[1, piece], rows.at[1, piece], send_twin, rows_sem.at[1, piece], device_id=twin, device_id_type=MESH
            ).start()

        @pl.when(root & (core_c == b))
        def _():
            send_part(rows.at[b], piece, twin, send_twin)

        @pl.when(relay & (core_c == b))
        def _():
            beside_it = aside(far, h)

            @pl.when(jnp.logical_not(beside_it))
            def _():
                send_part(rows.at[b], piece, device(*across[0], 1), send_cross)

            @pl.when(beside_it & (h == 0))
            def _():
                send_part(rows.at[b], piece, device(*across[1], 1), send_cross)

            @pl.when(beside_it & (h == 1))
            def _():
                send_part(rows.at[b], piece, device(*across[2], 1), send_cross)

    def both(s, body):
        body(-s, True)

        @pl.when((s >= 1) & (s <= 3))
        def _():
            body(s, False)

    def ring(b, s, up, piece, last_up, skip):
        if up:

            @pl.when(((s < 3) | ((s == 3) & last_up)) & jnp.logical_not(skip & ((z + 1) % Z == z_of[b])))
            def _():
                send_row(b, piece, z_up)

            @pl.when((s == 0) & jnp.logical_not(skip & ((z + Z - 1) % Z == z_of[b])))
            def _():
                send_row(b, piece, z_down)
        else:

            @pl.when(((s < 3) | jnp.logical_not(last_up)) & jnp.logical_not(skip & ((z + Z - 1) % Z == z_of[b])))
            def _():
                send_row(b, piece, z_down)

    def exchanged(b, s, j):
        return (s == 0) | jnp.where(j == 0, z != z_of[1 - b], z == z_of[b])

    def gather(n):
        s, j = div(n, 2), mod(n, 2)
        h = 1 - j

        def body(far, up):
            for b in range(2):

                def act(b=b):
                    for u in range(SPLIT):
                        piece = piece_of(far, 0, h) + u

                        @pl.when(s >= 1)
                        def _():
                            wait_row(b, piece)

                        ring(b, s, up, piece, (j == 0) if b == 0 else (j == 1), False)

                        @pl.when(exchanged(b, s, j))
                        def _():
                            send_row(b, piece, mate)

                        pass_on(b, far, piece, h)

                if b == 0:
                    act()
                else:
                    pl.when(s >= 1)(act)

        @pl.when(n < STEPS)
        def _():
            both(s, body)

        def crossed(far, up):
            for b in range(2):

                @pl.when(z == z_of[b])
                def _():
                    for u in range(SPLIT):
                        piece = piece_of(far, 1, h) + u
                        wait_row(b, piece)
                        pass_on(b, far, piece, h)

        @pl.when((n >= LAG) & (n < STEPS + LAG))
        def _():
            both(s - LAG // 2, crossed)

    def deferred(act, spans):
        for b, (start, stop) in enumerate(spans):

            @pl.when(z == z_of[1 - b])
            def _():
                def one(far, carry):
                    @pl.when(far != Z)
                    def _():
                        for u in range(SPLIT):
                            act(b, far, u)

                    return carry

                lax.fori_loop(start, stop, one, 0)

    def gather_rest(s):
        def body(far, up):
            for b in range(2):
                for u in range(SPLIT):
                    piece = piece_of(far, 1, 0) + u

                    @pl.when(z != z_of[b])
                    def _():
                        wait_row(b, piece)

                    ring(b, s, up, piece, b == 0, True)

                    if b == 1:

                        @pl.when(z != z_of[b])
                        def _():
                            pass_on(b, far, piece, 0)

                @pl.when((z != z_of[b]) & ((s == 0) | (z != z_of[1 - b])))
                def _():
                    for u in range(SPLIT):
                        piece = piece_of(far, 1, 1) + u
                        wait_row(b, piece)

                        @pl.when((z_to[b] == z_of[1 - b]) & (s <= 2) & (far != 2 * b - 1))
                        def _():
                            send_row(b, piece, z_up if b == 1 else z_down)

                        if b == 1:
                            pass_on(b, far, piece, 1)

        z_to = ((z + Z - 1) % Z, (z + 1) % Z)
        both(s, body)

    lag = [HOP * (jnp.where(same, 0, 1) + (rel if h == 0 else (X - rel) % X)) for h in range(2)]
    other = jnp.logical_not(same)
    early = jnp.where(same, 0, 1)

    def forward(far, mates, h):
        beside_it = other & aside(far, h)
        entry = jnp.where(beside_it, 1, 0)
        two_ways = beside_it | among(far, TWO_WAYS[h])
        hop = mod(rel - entry + X, X) if h == 0 else mod(2 * X - entry - rel, X)

        @pl.when(jnp.logical_not(beside_it & (rel == 0)))
        def _():
            for u in range(SPLIT):
                piece = piece_of(far, mates, h) + u
                wait_part(piece)

                @pl.when(hop < jnp.where(two_ways, X - 2, X - 1))
                def _():
                    send_part(part, piece, x_down if h else x_up, send_x)

                @pl.when(two_ways & (hop == 0))
                def _():
                    send_part(part, piece, x_up if h else x_down, send_x)

                send_part(part, piece, twin, send_twin)

    def accept(far, mates, h):
        @pl.when(other & aside(far, h) & (rel == 0))
        def _():
            for u in range(SPLIT):
                piece = piece_of(far, mates, h) + u
                wait_part(piece)
                send_part(part, piece, twin, send_twin)

    def spread(n):
        for act, lags in ((forward, lag), (accept, [3 * HOP, 3 * HOP])):
            for h in range(2):
                m = n - lags[h]
                parity = mod(m + 64, 2)

                @pl.when((m >= 0) & (m < STEPS) & (parity == 1 - h))
                def _():
                    both(div(m, 2), lambda far, up: act(far, early, h))

                @pl.when((m >= LAG) & (m < STEPS + LAG) & (parity == 1 - h))
                def _():
                    both(div(m - LAG, 2), lambda far, up: act(far, 1 - early, h))

    def multiply(mates, far):
        ends = (far, jnp.where(far == 0, 4, -far))
        for end in ends:
            tile = piece_of(end, mates, 0)

            @pl.when(first)
            def _():
                for u in range(2 * SPLIT):
                    wait_part(tile + u)

            @pl.when(second & ((end != 0) | (mates != 0)))
            def _():
                for u in range(2 * SPLIT):
                    wait_row(1, tile + u)

        def tiles(ref, *lead):
            return jnp.concatenate(
                [ref[*lead, pl.ds(piece_of(end, mates, 0), 2 * SPLIT)].reshape(2 * HALF, DEPTH) for end in ends], axis=1
            )

        out_ref[...] += lax.dot_general(
            tiles(rows, core), tiles(part), (((1,), (1,)), ((), ())), preferred_element_type=jnp.float32
        )

    @pl.when(second)
    def _():
        for u in (*range(SPLIT, 2 * SPLIT), *range(SPLIT)):
            for to in (z_up, z_down, mate):
                send_row(1, own + u, to)

        @pl.when(root & (core_c == 1))
        def _():
            for u in range(2 * SPLIT):
                pltpu.make_async_copy(rows.at[1, own + u], part.at[own + u], part_sem.at[own + u]).start()

        @pl.when(relay & (core_c == 1))
        def _():
            for u in range(2 * SPLIT):
                send_part(rows.at[1], own + u, device(*across[0], 1), send_cross)

    lag_most = jnp.where(other & (rel == 0), 3 * HOP, jnp.maximum(lag[0], lag[1]))
    rest = STEPS - 2

    def step(n, carry):
        @pl.when(first & (n < STEPS + LAG))
        def _():
            gather(n)

        @pl.when(first & (n >= rest) & (n < rest + ROUNDS))
        def _():
            gather_rest(n - rest)

        @pl.when(first & (n == STEPS))
        def _():
            deferred(lambda b, far, u: send_row(b, piece_of(far, 0, 1) + u, mate), ((4, 7), (2, 5)))

        def late(b, far, u):
            piece = piece_of(far, 1, 1) + u
            wait_row(b, piece)
            if b == 1:
                pass_on(b, far, piece, 1)

        @pl.when(first & (n == STEPS + LAG - 1))
        def _():
            deferred(late, ((7, 12), (5, 10)))

        @pl.when(first & (n == STEPS + LAG))
        def _():
            deferred(late, ((4, 7), (2, 5)))

        @pl.when(second)
        def _():
            spread(n)

        m = jnp.where(first, n - FIRST_AT, n - lag_most - SECOND_AT)

        @pl.when(m == 0)
        def _():
            stat.wait()

        turn = jnp.full((), -1, jnp.int32)
        for i, turns in enumerate(zip(*ORDER)):
            now = jnp.where(first, turns[0], jnp.where(root, turns[3], jnp.where(z == z_of[0], turns[2], turns[1])))
            turn = jnp.where(m == i, now, turn)

        @pl.when(turn >= 0)
        def _():
            multiply(div(turn, 4), mod(turn, 4))

        return carry

    lax.fori_loop(0, STEPS + LAG + 4 * HOP + 8, step, 0)

    def drain(sem, count):
        half = rows.at[:, pl.ds(0, count // 2 * SPLIT)]
        pltpu.make_async_copy(half, half, sem).wait()

    @pl.when(first)
    def _():
        half = rows.at[:, pl.ds(0, 27 * SPLIT)]
        pltpu.make_async_copy(half, half, send_rows).wait()

        @pl.when(root & (core_c == 0))
        def _():
            pltpu.make_async_copy(rows.at[:, pl.ds(0, 31 * SPLIT)], rows.at[:, pl.ds(0, 31 * SPLIT)], send_twin).wait()

        @pl.when(root & (core_c == 1))
        def _():
            pltpu.make_async_copy(rows.at[:, pl.ds(0, 30 * SPLIT)], rows.at[:, pl.ds(0, 30 * SPLIT)], send_twin).wait()

        @pl.when(jnp.logical_not(root))
        def _():
            drain(send_twin, 30)

        @pl.when(relay & (core_c == 0))
        def _():
            drain(send_cross, 32)

        @pl.when(relay & (core_c == 1))
        def _():
            drain(send_cross, 30)

    @pl.when(second)
    def _():
        drain(send_rows, 6)
        drain(send_twin, 32)

        @pl.when(relay & (core_c == 1))
        def _():
            drain(send_cross, 2)

        both_ways = 2 * sum(map(len, TWO_WAYS))
        up, down = (2 * len(distances) for distances in ASIDE)
        for at, count, beyond in (
            (0, 32 + both_ways, 32 + both_ways - up - down),
            (1, 16, 16 + up),
            (2, 32 - both_ways, 32 - both_ways),
            (3, 16, 16 + down),
        ):

            @pl.when(same & (rel == at))
            def _():
                drain(send_x, count)

            @pl.when(other & (rel == at))
            def _():
                drain(send_x, beyond)


def local(statistic, gradient):
    return pl.pallas_call(
        kernel,
        out_shape=jax.ShapeDtypeStruct(statistic.shape, jnp.float32),
        in_specs=[pl.BlockSpec(memory_space=pltpu.HBM)] * 2,
        out_specs=pl.BlockSpec(memory_space=pltpu.VMEM),
        scratch_shapes=[
            pltpu.VMEM((2, 2 * SPLIT * TILES, PIECE, DEPTH), jnp.bfloat16),
            pltpu.VMEM((2 * SPLIT * TILES, PIECE, DEPTH), jnp.bfloat16),
            pltpu.SemaphoreType.DMA((2 * SPLIT,)),
            pltpu.SemaphoreType.DMA,
            pltpu.SemaphoreType.DMA((2, 2 * SPLIT * TILES)),
            pltpu.SemaphoreType.DMA((2 * SPLIT * TILES,)),
            pltpu.SemaphoreType.DMA,
            pltpu.SemaphoreType.DMA,
            pltpu.SemaphoreType.DMA,
            pltpu.SemaphoreType.DMA,
        ],
        compiler_params=pltpu.CompilerParams(collective_id=0, has_side_effects=True, vmem_limit_bytes=48 << 20),
        cost_estimate=pl.CostEstimate(flops=2 * 1024 * 1024 * 4096, bytes_accessed=9 << 20, transcendentals=0),
        name="shampoo",
    )(statistic, gradient)


def solution(mesh):
    spec = P("row", "col")
    return jax.shard_map(local, mesh=mesh, in_specs=(spec, spec), out_specs=spec, check_vma=False)
```

```python
import functools

import jax
import jax.numpy as jnp
from jax import lax
from jax.experimental import pallas as pl
from jax.experimental.pallas import tpu as pltpu
from jax.sharding import PartitionSpec as P

MESH = pl.DeviceIdType.MESH
X, Y, Z = 4, 4, 8
TILES = 16
HALF = 512
DEPTH = 256
ROUNDS = 5
STEPS = 2 * ROUNDS
LAG = 2
ASIDE = ((1, 2, 3), (1, 2, 6))
TWO_WAYS = ((4, 5), (4,))
HOP = 2
SPLIT = 2
PIECE = HALF // SPLIT
FIRST_AT, SECOND_AT = 11, 5
ORDER = (
    (1, 2, 5, 6, 3, 7, 0, 4, -1, -1, -1, -1, -1, -1, -1),
    (1, 5, 2, 6, 3, 7, 0, 4, -1, -1, -1, -1, -1, -1, -1),
    (1, -1, 2, -1, 3, -1, 0, 5, 6, 7, 4, -1, -1, -1, -1),
    (-1, -1, -1, -1, -1, -1, -1, 1, 2, 3, 0, 5, 6, 7, 4),
)


def div(a, b):
    return lax.div(a, jnp.int32(b))


def mod(a, b):
    return lax.rem(a, jnp.int32(b))


def device(x, y, z, core):
    return (x * 4 + (y // 2) * 2 + core, (y % 2) * Z + z)


def kernel(stat_ref, grad_ref, out_ref, rows, part, own_sem, stat_sem, rows_sem, part_sem, send_rows, send_twin, send_x, send_cross):
    r, c = lax.axis_index("row"), lax.axis_index("col")
    x, yh, core = r // 4, (r // 2) % 2, r % 2
    yl, z = c // Z, c % Z
    y = 2 * yh + yl
    first, second = core == 0, core == 1

    x_c, yh_c, core_c = c // 4, (c // 2) % 2, c % 2
    rel = (x - x_c + X) % X
    same = yh == yh_c
    root = same & (rel == 0)

    z_up, z_down = (x, y, (z + 1) % Z), (x, y, (z + Z - 1) % Z)
    mate = (x, 2 * yh + 1 - yl, z)
    twin = device(x, y, z, 1 - core)
    x_up, x_down = device((x + 1) % X, y, z, core), device((x + X - 1) % X, y, z, core)

    x_m = (1 - yl) * 2 + z // 4
    relay = same & (x == x_m)
    z_of = [(x % 2) * 4 + yh * 2 + b for b in range(2)]
    across = [((x + d) % X, 2 * (1 - yh) + 1 - yl, z) for d in (0, 1, X - 1)]

    own = 2 * SPLIT * c
    load = [
        pltpu.make_async_copy(grad_ref.at[pl.ds(u * PIECE, PIECE)], rows.at[core, own + u], own_sem.at[u]) for u in range(2 * SPLIT)
    ]
    for copy in load:
        copy.start()
    stat = pltpu.make_async_copy(stat_ref, out_ref, stat_sem)
    stat.start()

    barrier = pltpu.get_barrier_semaphore()

    def greet(others):
        for other in others:
            pl.semaphore_signal(barrier, inc=1, device_id=other, device_id_type=MESH)
        pl.semaphore_wait(barrier, len(others))

    beside = [device(*at, 0) for at in (z_up, z_down, mate)]

    @pl.when(first)
    def _():
        greet([twin, *beside, *[device(*at, 1) for at in (z_up, z_down, mate, *across)]])

    @pl.when(second)
    def _():
        greet([twin, *beside, x_up, x_down, *[device(*at, k) for at in across for k in range(2)]])

    for copy in load:
        copy.wait()

    def send_row(b, piece, to):
        pltpu.make_async_remote_copy(
            rows.at[b, piece], rows.at[b, piece], send_rows, rows_sem.at[b, piece], device_id=device(*to, 0), device_id_type=MESH
        ).start()

    def send_part(source, piece, to, sem):
        pltpu.make_async_remote_copy(source.at[piece], part.at[piece], sem, part_sem.at[piece], device_id=to, device_id_type=MESH).start()

    def wait_row(b, piece):
        pltpu.make_async_copy(rows.at[b, piece], rows.at[b, piece], rows_sem.at[b, piece]).wait()

    def wait_part(piece):
        pltpu.make_async_copy(part.at[piece], part.at[piece], part_sem.at[piece]).wait()

    def piece_of(far, mates, h):
        return SPLIT * (2 * (mod(yl + mates, 2) * Z + mod(z + far + Z, Z)) + h)

    def among(far, distances):
        return functools.reduce(jnp.logical_or, [(far == d) | (far == d - Z) for d in distances], False)

    def aside(far, h):
        if isinstance(h, int):
            return among(far, ASIDE[h])
        return jnp.where(h == 0, among(far, ASIDE[0]), among(far, ASIDE[1]))

    def pass_on(b, far, piece, h):
        if b == 1:
            pltpu.make_async_remote_copy(
                rows.at[1, piece], rows.at[1, piece], send_twin, rows_sem.at[1, piece], device_id=twin, device_id_type=MESH
            ).start()

        @pl.when(root & (core_c == b))
        def _():
            send_part(rows.at[b], piece, twin, send_twin)

        @pl.when(relay & (core_c == b))
        def _():
            beside_it = aside(far, h)

            @pl.when(jnp.logical_not(beside_it))
            def _():
                send_part(rows.at[b], piece, device(*across[0], 1), send_cross)

            @pl.when(beside_it & (h == 0))
            def _():
                send_part(rows.at[b], piece, device(*across[1], 1), send_cross)

            @pl.when(beside_it & (h == 1))
            def _():
                send_part(rows.at[b], piece, device(*across[2], 1), send_cross)

    def both(s, body):
        body(-s, True)

        @pl.when((s >= 1) & (s <= 3))
        def _():
            body(s, False)

    def ring(b, s, up, piece, last_up, skip):
        if up:

            @pl.when(((s < 3) | ((s == 3) & last_up)) & jnp.logical_not(skip & ((z + 1) % Z == z_of[b])))
            def _():
                send_row(b, piece, z_up)

            @pl.when((s == 0) & jnp.logical_not(skip & ((z + Z - 1) % Z == z_of[b])))
            def _():
                send_row(b, piece, z_down)
        else:

            @pl.when(((s < 3) | jnp.logical_not(last_up)) & jnp.logical_not(skip & ((z + Z - 1) % Z == z_of[b])))
            def _():
                send_row(b, piece, z_down)

    def exchanged(b, s, j):
        return (s == 0) | jnp.where(j == 0, z != z_of[1 - b], z == z_of[b])

    def gather(n):
        s, j = div(n, 2), mod(n, 2)
        h = 1 - j

        def body(far, up):
            for b in range(2):

                def act(b=b):
                    for u in range(SPLIT):
                        piece = piece_of(far, 0, h) + u

                        @pl.when(s >= 1)
                        def _():
                            wait_row(b, piece)

                        pass_on(b, far, piece, h)

                        ring(b, s, up, piece, (j == 0) if b == 0 else (j == 1), False)

                        @pl.when(exchanged(b, s, j))
                        def _():
                            send_row(b, piece, mate)

                if b == 0:
                    act()
                else:
                    pl.when(s >= 1)(act)

        @pl.when(n < STEPS)
        def _():
            both(s, body)

        def crossed(far, up):
            for b in range(2):

                @pl.when(z == z_of[b])
                def _():
                    for u in range(SPLIT):
                        piece = piece_of(far, 1, h) + u
                        wait_row(b, piece)
                        pass_on(b, far, piece, h)

        @pl.when((n >= LAG) & (n < STEPS + LAG))
        def _():
            both(s - LAG // 2, crossed)

    def deferred(act, spans):
        for b, (start, stop) in enumerate(spans):

            @pl.when(z == z_of[1 - b])
            def _():
                def one(far, carry):
                    @pl.when(far != Z)
                    def _():
                        for u in range(SPLIT):
                            act(b, far, u)

                    return carry

                lax.fori_loop(start, stop, one, 0)

    def gather_rest(s):
        def body(far, up):
            for b in range(2):
                for u in range(SPLIT):
                    piece = piece_of(far, 1, 0) + u

                    @pl.when(z != z_of[b])
                    def _():
                        wait_row(b, piece)

                    ring(b, s, up, piece, b == 0, True)

                    if b == 1:

                        @pl.when(z != z_of[b])
                        def _():
                            pass_on(b, far, piece, 0)

                @pl.when((z != z_of[b]) & ((s == 0) | (z != z_of[1 - b])))
                def _():
                    for u in range(SPLIT):
                        piece = piece_of(far, 1, 1) + u
                        wait_row(b, piece)

                        @pl.when((z_to[b] == z_of[1 - b]) & (s <= 2) & (far != 2 * b - 1))
                        def _():
                            send_row(b, piece, z_up if b == 1 else z_down)

                        if b == 1:
                            pass_on(b, far, piece, 1)

        z_to = ((z + Z - 1) % Z, (z + 1) % Z)
        both(s, body)

    lag = [HOP * (jnp.where(same, 0, 1) + (rel if h == 0 else (X - rel) % X)) for h in range(2)]
    other = jnp.logical_not(same)
    early = jnp.where(same, 0, 1)

    def forward(far, mates, h):
        beside_it = other & aside(far, h)
        entry = jnp.where(beside_it, 1, 0)
        two_ways = beside_it | among(far, TWO_WAYS[h])
        hop = mod(rel - entry + X, X) if h == 0 else mod(2 * X - entry - rel, X)

        @pl.when(jnp.logical_not(beside_it & (rel == 0)))
        def _():
            for u in range(SPLIT):
                piece = piece_of(far, mates, h) + u
                wait_part(piece)

                @pl.when(hop < jnp.where(two_ways, X - 2, X - 1))
                def _():
                    send_part(part, piece, x_down if h else x_up, send_x)

                @pl.when(two_ways & (hop == 0))
                def _():
                    send_part(part, piece, x_up if h else x_down, send_x)

                send_part(part, piece, twin, send_twin)

    def accept(far, mates, h):
        @pl.when(other & aside(far, h) & (rel == 0))
        def _():
            for u in range(SPLIT):
                piece = piece_of(far, mates, h) + u
                wait_part(piece)
                send_part(part, piece, twin, send_twin)

    def spread(n):
        for act, lags in ((forward, lag), (accept, [3 * HOP, 3 * HOP])):
            for h in range(2):
                m = n - lags[h]
                parity = mod(m + 64, 2)

                @pl.when((m >= 0) & (m < STEPS) & (parity == 1 - h))
                def _():
                    both(div(m, 2), lambda far, up: act(far, early, h))

                @pl.when((m >= LAG) & (m < STEPS + LAG) & (parity == 1 - h))
                def _():
                    both(div(m - LAG, 2), lambda far, up: act(far, 1 - early, h))

    def multiply(mates, far):
        ends = (far, jnp.where(far == 0, 4, -far))
        for end in ends:
            tile = piece_of(end, mates, 0)

            @pl.when(first)
            def _():
                for u in range(2 * SPLIT):
                    wait_part(tile + u)

            @pl.when(second & ((end != 0) | (mates != 0)))
            def _():
                for u in range(2 * SPLIT):
                    wait_row(1, tile + u)

        def tiles(ref, *lead):
            return jnp.concatenate(
                [ref[*lead, pl.ds(piece_of(end, mates, 0), 2 * SPLIT)].reshape(2 * HALF, DEPTH) for end in ends], axis=1
            )

        out_ref[...] += lax.dot_general(
            tiles(rows, core), tiles(part), (((1,), (1,)), ((), ())), preferred_element_type=jnp.float32
        )

    @pl.when(second)
    def _():
        for u in (*range(SPLIT, 2 * SPLIT), *range(SPLIT)):
            for to in (z_up, z_down, mate):
                send_row(1, own + u, to)

        @pl.when(root & (core_c == 1))
        def _():
            for u in range(2 * SPLIT):
                pltpu.make_async_copy(rows.at[1, own + u], part.at[own + u], part_sem.at[own + u]).start()

        @pl.when(relay & (core_c == 1))
        def _():
            for u in range(2 * SPLIT):
                send_part(rows.at[1], own + u, device(*across[0], 1), send_cross)

    lag_most = jnp.where(other & (rel == 0), 3 * HOP, jnp.maximum(lag[0], lag[1]))
    rest = STEPS - 2

    def step(n, carry):
        @pl.when(first & (n < STEPS + LAG))
        def _():
            gather(n)

        @pl.when(first & (n >= rest) & (n < rest + ROUNDS))
        def _():
            gather_rest(n - rest)

        @pl.when(first & (n == STEPS))
        def _():
            deferred(lambda b, far, u: send_row(b, piece_of(far, 0, 1) + u, mate), ((4, 7), (2, 5)))

        def late(b, far, u):
            piece = piece_of(far, 1, 1) + u
            wait_row(b, piece)
            if b == 1:
                pass_on(b, far, piece, 1)

        @pl.when(first & (n == STEPS + LAG - 1))
        def _():
            deferred(late, ((7, 12), (5, 10)))

        @pl.when(first & (n == STEPS + LAG))
        def _():
            deferred(late, ((4, 7), (2, 5)))

        @pl.when(second)
        def _():
            spread(n)

        m = jnp.where(first, n - FIRST_AT, n - lag_most - SECOND_AT)

        @pl.when(m == 0)
        def _():
            stat.wait()

        turn = jnp.full((), -1, jnp.int32)
        for i, turns in enumerate(zip(*ORDER)):
            now = jnp.where(first, turns[0], jnp.where(root, turns[3], jnp.where(z == z_of[0], turns[2], turns[1])))
            turn = jnp.where(m == i, now, turn)

        @pl.when(turn >= 0)
        def _():
            multiply(div(turn, 4), mod(turn, 4))

        return carry

    lax.fori_loop(0, STEPS + LAG + 4 * HOP + 8, step, 0)

    def drain(sem, count):
        half = rows.at[:, pl.ds(0, count // 2 * SPLIT)]
        pltpu.make_async_copy(half, half, sem).wait()

    @pl.when(first)
    def _():
        half = rows.at[:, pl.ds(0, 27 * SPLIT)]
        pltpu.make_async_copy(half, half, send_rows).wait()

        @pl.when(root & (core_c == 0))
        def _():
            pltpu.make_async_copy(rows.at[:, pl.ds(0, 31 * SPLIT)], rows.at[:, pl.ds(0, 31 * SPLIT)], send_twin).wait()

        @pl.when(root & (core_c == 1))
        def _():
            pltpu.make_async_copy(rows.at[:, pl.ds(0, 30 * SPLIT)], rows.at[:, pl.ds(0, 30 * SPLIT)], send_twin).wait()

        @pl.when(jnp.logical_not(root))
        def _():
            drain(send_twin, 30)

        @pl.when(relay & (core_c == 0))
        def _():
            drain(send_cross, 32)

        @pl.when(relay & (core_c == 1))
        def _():
            drain(send_cross, 30)

    @pl.when(second)
    def _():
        drain(send_rows, 6)
        drain(send_twin, 32)

        @pl.when(relay & (core_c == 1))
        def _():
            drain(send_cross, 2)

        both_ways = 2 * sum(map(len, TWO_WAYS))
        up, down = (2 * len(distances) for distances in ASIDE)
        for at, count, beyond in (
            (0, 32 + both_ways, 32 + both_ways - up - down),
            (1, 16, 16 + up),
            (2, 32 - both_ways, 32 - both_ways),
            (3, 16, 16 + down),
        ):

            @pl.when(same & (rel == at))
            def _():
                drain(send_x, count)

            @pl.when(other & (rel == at))
            def _():
                drain(send_x, beyond)


def local(statistic, gradient):
    return pl.pallas_call(
        kernel,
        out_shape=jax.ShapeDtypeStruct(statistic.shape, jnp.float32),
        in_specs=[pl.BlockSpec(memory_space=pltpu.HBM)] * 2,
        out_specs=pl.BlockSpec(memory_space=pltpu.VMEM),
        scratch_shapes=[
            pltpu.VMEM((2, 2 * SPLIT * TILES, PIECE, DEPTH), jnp.bfloat16),
            pltpu.VMEM((2 * SPLIT * TILES, PIECE, DEPTH), jnp.bfloat16),
            pltpu.SemaphoreType.DMA((2 * SPLIT,)),
            pltpu.SemaphoreType.DMA,
            pltpu.SemaphoreType.DMA((2, 2 * SPLIT * TILES)),
            pltpu.SemaphoreType.DMA((2 * SPLIT * TILES,)),
            pltpu.SemaphoreType.DMA,
            pltpu.SemaphoreType.DMA,
            pltpu.SemaphoreType.DMA,
            pltpu.SemaphoreType.DMA,
        ],
        compiler_params=pltpu.CompilerParams(collective_id=0, has_side_effects=True, vmem_limit_bytes=48 << 20),
        cost_estimate=pl.CostEstimate(flops=2 * 1024 * 1024 * 4096, bytes_accessed=9 << 20, transcendentals=0),
        name="shampoo",
    )(statistic, gradient)


def solution(mesh):
    spec = P("row", "col")
    return jax.shard_map(local, mesh=mesh, in_specs=(spec, spec), out_specs=spec, check_vma=False)
```
